512 devices in a mesh: dp: 4 (over y_lo, core), ctx: 32 (over z, y_hi), tp: 4 (over x).
Axes of the slice: x: 4, y: 8 (y_hi: 4, y_lo: 2; y = y_hi * 2 + y_lo), z: 8, core: 2. Of those that a mesh axis runs over, the one named last changes fastest.
Arguments:
- queries: bfloat16 [16384, 4096], P(('dp', 'ctx'), 'tp'), parts along dimension 0, may hold values from -120 to 120
- keys: bfloat16 [16384, 512], P(('dp', 'ctx'), 'tp'), parts along dimension 0, may hold values from -12 to 12
- values: bfloat16 [16384, 512], P(('dp', 'ctx'), 'tp'), parts along dimension 0, may hold values from -20 to 20
- readout: bfloat16 [4096, 1536], P('tp'), may hold values from -8 to 8
- token_ids: int32 [16384], P(('dp', 'ctx')), parts along dimension 0, may hold values from 0 to 1535
- stored_logp: float32 [16384], P(('dp', 'ctx')), parts along dimension 0, may hold values from -12 to -0.5
- span_order: int32 [256], P('dp'), parts along dimension 0, may hold values from 0 to 63, each once
Outputs:
- attended: bfloat16 [16384, 4096], P(('dp', 'ctx'), 'tp'), parts along dimension 0
- log_ratio: float32 [16384], P(('dp', 'ctx')), parts along dimension 0
The draws below stay inside these ranges and needn't reach their ends.
There are 4 independent parts, one for each index of `dp`. The reference program is written for one: setup_inputs(seed, part) draws one part's arguments, and reference() takes and returns one part's arrays. A program takes and returns all parts, laid end to end along the dimension named above; an argument that names none is the same for every part. Nothing has to cross between parts.
Inputs may be any that keep to these rules, and one draw needn't show every extreme that they name: `span_order`: each block index appears in exactly one slot.
All inputs are finite; a program needn't handle non-finite values.
Results may differ from the reference program's by a relative error of at most 0.006.
Values may be sent and summed in bfloat16 or wider, within the bound.
No kernel may reach another device: no remote copies, remote signals or barrier semaphores. Data moves between devices by JAX's collectives and lax.ppermute only.
A program may use at most 64 MiB of HBM per device.

```python
import math
import jax
import jax.numpy as jnp
import numpy as np
from jax import lax

HEAD_SIZE = 128
QUERY_HEAD_COUNT = 32
KEY_VALUE_HEADS = 4
ROLLOUT_LENGTH = 4096
VOCAB = 1536
N_CTX = 32


def draw_queries(key, part):
    key = jax.random.fold_in(key, 1)
    query_group_ratio = QUERY_HEAD_COUNT // KEY_VALUE_HEADS
    perturbation_key = jax.random.fold_in(key, 0)
    complete_output = 1.5 * jnp.clip(jax.random.normal(perturbation_key, (ROLLOUT_LENGTH, KEY_VALUE_HEADS, query_group_ratio, HEAD_SIZE), jnp.float32), -6.0, 6.0)
    return jnp.clip(complete_output, -120.0, 120.0).reshape(ROLLOUT_LENGTH, QUERY_HEAD_COUNT * HEAD_SIZE).astype(jnp.bfloat16)


def draw_keys(key, part):
    key = jax.random.fold_in(key, 2)
    perturbation_key = jax.random.fold_in(key, 0)
    complete_output = jnp.clip(jax.random.normal(perturbation_key, (ROLLOUT_LENGTH, KEY_VALUE_HEADS, HEAD_SIZE), jnp.float32), -6.0, 6.0)
    return jnp.clip(complete_output, -12.0, 12.0).reshape(ROLLOUT_LENGTH, KEY_VALUE_HEADS * HEAD_SIZE).astype(jnp.bfloat16)


def draw_values(key, part):
    key = jax.random.fold_in(key, 3)
    perturbation_key, level_key = jax.random.split(key)
    per_row_scale = jnp.exp(jax.random.uniform(level_key, (ROLLOUT_LENGTH,), jnp.float32, math.log(0.3), math.log(3.0)))
    complete_output = jnp.clip(jax.random.normal(perturbation_key, (ROLLOUT_LENGTH, KEY_VALUE_HEADS, HEAD_SIZE), jnp.float32), -6.0, 6.0) * per_row_scale[:, None, None]
    return jnp.clip(complete_output, -20.0, 20.0).reshape(ROLLOUT_LENGTH, KEY_VALUE_HEADS * HEAD_SIZE).astype(jnp.bfloat16)


def draw_readout(key, part):
    key = jax.random.fold_in(key, 4)
    perturbation_key, column_key = jax.random.split(key, 2)
    features = QUERY_HEAD_COUNT * HEAD_SIZE
    column_scale = jnp.exp(jax.random.uniform(column_key, (VOCAB,), jnp.float32, math.log(0.3), math.log(3.0)))
    complete_output = 0.4 * jnp.clip(jax.random.normal(perturbation_key, (features, VOCAB), jnp.float32), -6.0, 6.0) * column_scale[None, :]
    return jnp.clip(complete_output, -8.0, 8.0).astype(jnp.bfloat16)


def set_ends(array, rng, low, largest):
    longest = array.shape.index(max(array.shape))
    spots = []
    for shift in (0, 1):
        where = [jax.random.randint(jax.random.fold_in(rng, axis), (), 0, length) for axis, length in enumerate(array.shape)]
        where[longest] = (where[longest] + shift) % array.shape[longest]
        spots.append(tuple(where))
    return array.at[spots[0]].set(low).at[spots[1]].set(largest)


def block_scale(own_key, extent, pieces, least, top_value):
    def one(dim, shards_of):
        draws = jax.random.uniform(jax.random.fold_in(jax.random.fold_in(own_key, 6), dim), (shards_of,), jnp.float32, least / len(pieces), top_value / len(pieces))
        return jnp.repeat(jnp.exp(draws), extent[dim] // shards_of).reshape((-1,) + (1,) * (len(extent) - dim - 1))

    gain = one(*pieces[0])
    for cut in pieces[1:]:
        gain = gain * one(*cut)
    return gain


def cumulative_ranks(count, skew):
    weights = [(1 << 20) // math.isqrt(grade ** skew) + 1 for grade in range(1, count + 1)]
    deviation = 1 + sum(weights) // (1 << 30)
    return np.cumsum(np.array([max(1, weight // deviation) for weight in weights]))


def ranked(key, dims, number_of, slope):
    table = cumulative_ranks(number_of, slope)
    ticket = jax.random.randint(jax.random.fold_in(key, 1), dims, 0, int(table[number_of - 1]))
    rank = jnp.searchsorted(jnp.asarray(table, jnp.int32), ticket, side="right")
    return jax.random.permutation(jax.random.fold_in(key, 2), number_of)[rank].astype(jnp.int32)


def setup_inputs(seed: int = 0, part: int = 0) -> dict:
    key_of = jax.random.split(jax.random.key(seed), 8)
    own_keys = jax.random.split(jax.random.fold_in(key_of[7], part), 8)
    return {
        "queries": draw_queries(jax.random.fold_in(jax.random.fold_in(key_of[7], part), 71), part),
        "keys": draw_keys(jax.random.fold_in(jax.random.fold_in(key_of[7], part), 71), part),
        "values": draw_values(jax.random.fold_in(jax.random.fold_in(key_of[7], part), 71), part),
        "readout": draw_readout(jax.random.fold_in(key_of[7], 71), part),
        "token_ids": set_ends(ranked(own_keys[4], (ROLLOUT_LENGTH,), VOCAB, 2), jax.random.fold_in(own_keys[4], 3), 0, VOCAB - 1).astype(jnp.int32),
        "stored_logp": jnp.clip(-12.0 + 11.5 * jax.random.uniform(own_keys[5], (ROLLOUT_LENGTH,), jnp.float32) ** block_scale(own_keys[5], (ROLLOUT_LENGTH,), ((0, 32),), -0.2, 0.2), -12.0, -0.5),
        "span_order": jax.random.permutation(own_keys[6], 2 * N_CTX).astype(jnp.int32),
    }


floor_value = -1e+30

def reference(queries, keys, values, readout, token_ids, stored_logp, span_order):
    halved_row_count = ROLLOUT_LENGTH // (2 * N_CTX)
    total_slot_count = 2 * N_CTX
    query_group_ratio = QUERY_HEAD_COUNT // KEY_VALUE_HEADS
    offsets = jnp.arange(halved_row_count, dtype=jnp.int32)
    positions = (span_order.astype(jnp.int32)[:, None] * halved_row_count + offsets[None, :]).reshape(-1).astype(jnp.int32)
    key_single_precision = keys.astype(jnp.float32).reshape(ROLLOUT_LENGTH, KEY_VALUE_HEADS, HEAD_SIZE)
    value_single_precision = values.astype(jnp.float32).reshape(ROLLOUT_LENGTH, KEY_VALUE_HEADS, HEAD_SIZE)
    query_slot_indices = queries.reshape(total_slot_count, halved_row_count, KEY_VALUE_HEADS, query_group_ratio, HEAD_SIZE)
    slot_positions = positions.reshape(total_slot_count, halved_row_count)
    score_scale = 1.0 / math.sqrt(HEAD_SIZE)

    def attend_slot(inputs):
        query_block, query_pos = inputs
        scores = jnp.einsum('qgrd,kgd->qgrk', query_block.astype(jnp.float32), key_single_precision) * score_scale
        visible = positions[None, None, None, :] <= query_pos[:, None, None, None]
        scores = jnp.where(visible, scores, floor_value)
        highest = lax.optimization_barrier(jnp.max(scores, axis=-1, keepdims=True))
        weights = jnp.where(visible, jnp.exp(scores - highest), 0.0)
        totals = lax.optimization_barrier(jnp.sum(weights, axis=-1))
        rounded = lax.optimization_barrier(weights.astype(jnp.bfloat16)).astype(jnp.float32)
        mixed = jnp.einsum('qgrk,kgd->qgrd', rounded, value_single_precision)
        return (mixed / totals[..., None]).reshape(halved_row_count, QUERY_HEAD_COUNT * HEAD_SIZE).astype(jnp.bfloat16)
    attended = lax.map(attend_slot, (query_slot_indices, slot_positions)).reshape(ROLLOUT_LENGTH, QUERY_HEAD_COUNT * HEAD_SIZE)
    logits = jnp.dot(attended, readout, preferred_element_type=jnp.float32)
    highest = lax.optimization_barrier(jnp.max(logits, axis=1))
    log_norm = highest + jnp.log(lax.optimization_barrier(jnp.sum(jnp.exp(logits - highest[:, None]), axis=1)))
    target = jnp.take_along_axis(logits, token_ids[:, None], axis=1)[:, 0]
    return (attended, target - log_norm - stored_logp)
```

```python
import functools
import math

import jax
import jax.numpy as jnp
from jax import lax
from jax.experimental import pallas as pl
from jax.experimental.pallas import tpu as pltpu
from jax.sharding import PartitionSpec as P

HEAD = 128
Z = 8
Y = 4
TP = 4
SPAN = 64
ROW_TILE = 256
EXP2_SCALE = math.log2(math.e) / math.sqrt(HEAD)
MASKED = -1e30
COST = 4
Y_GROUPS = [[z * Y + y for y in range(Y)] for z in range(Z)]


def swap_z(x, odd):
    pairs = []
    for z in range(Z):
        partner = (z + (1 if z % 2 == odd else -1)) % Z
        pairs += [(z * Y + y, partner * Y + y) for y in range(Y)]
    return lax.ppermute(x, "ctx", pairs)


VMEM = pl.BlockSpec(memory_space=pltpu.VMEM)
SMEM = pl.BlockSpec(memory_space=pltpu.SMEM)
HBM = pl.BlockSpec(memory_space=pltpu.HBM)


def block(dz):
    return [(dz, y) for y in range(Y)]


def ring_order():
    order = block(0)
    for step in range(1, Z // 2):
        dz = step if step % 2 else -step
        order += block(dz) + block(-dz)
    return order + block(Z // 2)


def pack_kernel(k_ref, v_ref, out_ref, sems):
    copies = []
    for j in range(Y):
        copies.append(pltpu.make_async_copy(k_ref, out_ref.at[j, :, pl.ds(0, HEAD)], sems.at[2 * j]))
        copies.append(pltpu.make_async_copy(v_ref, out_ref.at[j, :, pl.ds(HEAD, HEAD)], sems.at[2 * j + 1]))
    for copy in copies:
        copy.start()
    for copy in copies:
        copy.wait()


def pack(keys, values):
    return pl.pallas_call(
        pack_kernel,
        out_shape=jax.ShapeDtypeStruct((Y, keys.shape[0], 2 * HEAD), keys.dtype),
        in_specs=[HBM] * 2,
        out_specs=VMEM,
        scratch_shapes=[pltpu.SemaphoreType.DMA((2 * Y,))],
        name="pack",
    )(keys, values)


def prep_kernel(ids, order, q_ref, q_all, bias_ref, sem):
    heads = q_ref.shape[1] // HEAD
    rows = q_ref.shape[0]
    copies = []
    for h in range(heads):
        copies.append(
            pltpu.make_async_copy(
                q_ref.at[:, pl.ds(h * HEAD, HEAD)], q_all.at[pl.ds(h * rows, rows), pl.ds(0, HEAD)], sem.at[h]
            )
        )
        copies[h].start()
    eye = (
        lax.broadcasted_iota(jnp.int32, (HEAD, HEAD), 0) == lax.broadcasted_iota(jnp.int32, (HEAD, HEAD), 1)
    ).astype(jnp.bfloat16)
    for h in range(heads):
        q_all[h * rows : (h + 1) * rows, HEAD:] = eye
    me = ids[0]
    z = me // Y
    sign = 1 - 2 * (z % 2)
    row = lax.broadcasted_iota(jnp.int32, (SPAN, 2 * SPAN), 1)
    key = lax.broadcasted_iota(jnp.int32, (SPAN, 2 * SPAN), 0)
    row_pos = jnp.where(row < SPAN, order[2 * me] * SPAN + row, order[2 * me + 1] * SPAN + row - SPAN)
    lead = row_pos - key
    for i, (dz, y) in enumerate(ring_order()):
        src = ((z + sign * dz + Z) % Z) * Y + y
        for half in range(2):
            at = (2 * i + half) * SPAN
            visible = lead >= order[2 * src + half] * SPAN
            bias_ref[at : at + SPAN, :] = jnp.where(visible, 0.0, MASKED).astype(jnp.bfloat16)
    for copy in copies:
        copy.wait()


def prep(ids, order, queries):
    rows, width = queries.shape
    return pl.pallas_call(
        prep_kernel,
        out_shape=[
            jax.ShapeDtypeStruct((rows * (width // HEAD), 2 * HEAD), jnp.bfloat16),
            jax.ShapeDtypeStruct((Z * Y * rows, rows), jnp.bfloat16),
        ],
        in_specs=[SMEM, SMEM, HBM],
        out_specs=[VMEM, VMEM],
        scratch_shapes=[pltpu.SemaphoreType.DMA((width // HEAD,))],
        cost_estimate=pl.CostEstimate(flops=2 * 10**9, bytes_accessed=2 * 2**20, transcendentals=0),
        compiler_params=pltpu.CompilerParams(vmem_limit_bytes=16 * 2**20),
        name="prep",
    )(ids, order, queries)


def attend_kernel(start, n_kv, first, last, q_all, bias_ref, *refs):
    kv_refs, refs = refs[:n_kv], refs[n_kv:]
    if not first:
        acc_in, peak_in, refs = refs[0], refs[1], refs[2:]
    if last:
        w_ref, att_ref, part_ref = refs
    else:
        acc_out, peak_out = refs
    total, rows = q_all.shape[0], bias_ref.shape[1]
    k = jnp.concatenate([r[:, :, :HEAD].reshape(-1, HEAD) for r in kv_refs], axis=0)
    v = jnp.concatenate([r[:, :, HEAD:].reshape(-1, HEAD) for r in kv_refs], axis=0)
    k_ext = jnp.concatenate([k, bias_ref[start : start + k.shape[0], :]], axis=1)
    v_ext = jnp.concatenate([v, jnp.ones_like(v)], axis=1)
    for r in range(total // ROW_TILE):
        at = slice(r * ROW_TILE, (r + 1) * ROW_TILE)
        s = lax.dot_general(q_all[at, :], k_ext, (((1,), (1,)), ((), ())), preferred_element_type=jnp.float32)
        peak = jnp.max(s, axis=1, keepdims=True)
        if not first:
            old = peak_in[at, :1]
            peak = jnp.maximum(old, peak)
        p = jnp.exp2((s - peak) * EXP2_SCALE).astype(jnp.bfloat16)
        acc = jnp.dot(p, v_ext, preferred_element_type=jnp.float32)
        if not first:
            acc = acc + acc_in[at, :] * jnp.exp2((old - peak) * EXP2_SCALE)
        if last:
            att = (acc[:, :HEAD] / acc[:, HEAD:]).astype(jnp.bfloat16)
            for i in range(ROW_TILE // rows):
                h = r * ROW_TILE // rows + i
                att_ref[:, h * HEAD : (h + 1) * HEAD] = att[i * rows : (i + 1) * rows, :]
        else:
            acc_out[at, :] = acc
            peak_out[at, :] = jnp.broadcast_to(peak, (ROW_TILE, HEAD))
    if last:
        logits = jnp.dot(att_ref[...], w_ref[...], preferred_element_type=jnp.float32)
        part = rows // TP
        for t in range(TP):
            part_ref[t] = logits[t * part : (t + 1) * part, :].astype(jnp.bfloat16)


def attend(q_all, bias, kvs, start, state=None, readout=None):
    first, last = state is None, readout is not None
    total, rows = q_all.shape[0], bias.shape[1]
    keys = sum(kv.shape[0] * kv.shape[1] for kv in kvs)
    f32, b16 = jnp.float32, jnp.bfloat16
    args = [q_all, bias, *kvs]
    if not first:
        args += list(state)
    if last:
        vocab = readout.shape[1]
        args.append(readout)
        out = [
            jax.ShapeDtypeStruct((rows, total // rows * HEAD), b16),
            jax.ShapeDtypeStruct((TP, rows // TP, vocab), b16),
        ]
    else:
        out = [jax.ShapeDtypeStruct((total, 2 * HEAD), f32), jax.ShapeDtypeStruct((total, HEAD), f32)]
    return pl.pallas_call(
        functools.partial(attend_kernel, start, len(kvs), first, last),
        out_shape=out,
        in_specs=[VMEM] * len(args),
        out_specs=[VMEM] * len(out),
        cost_estimate=pl.CostEstimate(
            flops=COST * 4 * total * keys * 2 * HEAD, bytes_accessed=4 * 2**20, transcendentals=total * keys
        ),
        compiler_params=pltpu.CompilerParams(vmem_limit_bytes=24 * 2**20),
        name="attend_last" if last else "attend",
    )(*args)


def ratio_kernel(ids, part_ref, tok_ref, logp_ref, out_ref):
    f32 = jnp.float32
    _, part, vocab = part_ref.shape
    x = part_ref[0].astype(f32)
    for t in range(1, TP):
        x = x + part_ref[t].astype(f32)
    rows = tok_ref.shape[1]
    start = ids[1] * part
    mine = (
        lax.broadcasted_iota(jnp.int32, (part, rows), 0) + start
        == lax.broadcasted_iota(jnp.int32, (part, rows), 1)
    )
    token = jnp.sum(jnp.where(mine, tok_ref[...].astype(f32), 0.0), axis=1, keepdims=True).astype(jnp.int32)
    hit = lax.broadcasted_iota(jnp.int32, (part, vocab), 1) == token
    target = jnp.sum(jnp.where(hit, x, 0.0), axis=1, keepdims=True)
    peak = jnp.max(x, axis=1, keepdims=True)
    mass = jnp.sum(jnp.exp(x - peak), axis=1, keepdims=True)
    ratio = target - (peak + jnp.log(mass))
    mine_row = jnp.sum(jnp.where(mine, ratio - logp_ref[...], 0.0), axis=0, keepdims=True)
    out_ref[...] = jnp.broadcast_to(mine_row[None], out_ref.shape)


def body(queries, keys, values, readout, token_ids, stored_logp, span_order):
    rows = queries.shape[0]
    ids = jnp.stack([lax.axis_index("ctx"), lax.axis_index("tp")]).astype(jnp.int32)
    q_all, bias = prep(ids, span_order, queries)

    kv = lax.all_to_all(pack(keys, values), "ctx", 0, 0, axis_index_groups=Y_GROUPS, tiled=True)
    a, b = swap_z(kv, 0), swap_z(kv, 1)
    start = Y * rows
    state = attend(q_all, bias, [kv], 0)
    for step in range(1, Z // 2):
        now = [a, b]
        if step == Z // 2 - 1:
            a, b = a[: Y // 2], b[Y // 2 :]
        a, b = swap_z(a, step % 2), swap_z(b, 1 - step % 2)
        state = attend(q_all, bias, now, start, state)
        start += 2 * Y * rows
    attended, parts = attend(q_all, bias, [a, b], start, state, readout)

    parts = lax.all_to_all(parts, "tp", 0, 0, tiled=True)
    args = [parts, token_ids.reshape(1, rows), stored_logp.reshape(1, rows)]
    ratio = pl.pallas_call(
        ratio_kernel,
        out_shape=jax.ShapeDtypeStruct((TP, 1, rows), jnp.float32),
        in_specs=[SMEM] + [VMEM] * len(args),
        out_specs=VMEM,
        name="ratio",
    )(ids, *args)
    ratio = lax.all_to_all(ratio, "tp", 0, 0, tiled=True)
    return attended, jnp.sum(ratio, axis=(0, 1))


def solution(mesh):
    return jax.shard_map(
        body,
        mesh=mesh,
        in_specs=(
            P(("dp", "ctx"), "tp"),
            P(("dp", "ctx"), "tp"),
            P(("dp", "ctx"), "tp"),
            P("tp", None),
            P(("dp", "ctx")),
            P(("dp", "ctx")),
            P("dp"),
        ),
        out_specs=(P(("dp", "ctx"), "tp"), P(("dp", "ctx"))),
        check_vma=False,
    )
```

```python
import functools
import math

import jax
import jax.numpy as jnp
from jax import lax
from jax.experimental import pallas as pl
from jax.experimental.pallas import tpu as pltpu
from jax.sharding import PartitionSpec as P

HEAD = 128
Z = 8
Y = 4
TP = 4
SPAN = 64
ROW_TILE = 256
EXP2_SCALE = math.log2(math.e) / math.sqrt(HEAD)
MASKED = -1e30
COST = 4
Y_GROUPS = [[z * Y + y for y in range(Y)] for z in range(Z)]


def swap_z(x, odd):
    pairs = []
    for z in range(Z):
        partner = (z + (1 if z % 2 == odd else -1)) % Z
        pairs += [(z * Y + y, partner * Y + y) for y in range(Y)]
    return lax.ppermute(x, "ctx", pairs)


VMEM = pl.BlockSpec(memory_space=pltpu.VMEM)
SMEM = pl.BlockSpec(memory_space=pltpu.SMEM)
HBM = pl.BlockSpec(memory_space=pltpu.HBM)


def block(dz):
    return [(dz, y) for y in range(Y)]


def ring_order():
    order = block(0)
    for step in range(1, Z // 2):
        dz = step if step % 2 else -step
        order += block(dz) + block(-dz)
    return order + block(Z // 2)


def pack_kernel(k_ref, v_ref, out_ref, sems):
    copies = [
        pltpu.make_async_copy(k_ref, out_ref.at[0, :, pl.ds(0, HEAD)], sems.at[0]),
        pltpu.make_async_copy(v_ref, out_ref.at[0, :, pl.ds(HEAD, HEAD)], sems.at[1]),
    ]
    for copy in copies:
        copy.start()
    for copy in copies:
        copy.wait()
    for j in range(1, Y):
        out_ref[j] = out_ref[0]


def pack(keys, values):
    return pl.pallas_call(
        pack_kernel,
        out_shape=jax.ShapeDtypeStruct((Y, keys.shape[0], 2 * HEAD), keys.dtype),
        in_specs=[HBM] * 2,
        out_specs=VMEM,
        scratch_shapes=[pltpu.SemaphoreType.DMA((2,))],
        name="pack",
    )(keys, values)


def prep_kernel(ids, order, q_ref, q_all, bias_ref, sem):
    heads = q_ref.shape[1] // HEAD
    rows = q_ref.shape[0]
    copies = []
    for h in range(heads):
        copies.append(
            pltpu.make_async_copy(
                q_ref.at[:, pl.ds(h * HEAD, HEAD)], q_all.at[pl.ds(h * rows, rows), pl.ds(0, HEAD)], sem.at[h]
            )
        )
        copies[h].start()
    eye = (
        lax.broadcasted_iota(jnp.int32, (HEAD, HEAD), 0) == lax.broadcasted_iota(jnp.int32, (HEAD, HEAD), 1)
    ).astype(jnp.bfloat16)
    for h in range(heads):
        q_all[h * rows : (h + 1) * rows, HEAD:] = eye
    me = ids[0]
    z = me // Y
    sign = 1 - 2 * (z % 2)
    row = lax.broadcasted_iota(jnp.int32, (SPAN, 2 * SPAN), 1)
    key = lax.broadcasted_iota(jnp.int32, (SPAN, 2 * SPAN), 0)
    row_pos = jnp.where(row < SPAN, order[2 * me] * SPAN + row, order[2 * me + 1] * SPAN + row - SPAN)
    lead = row_pos - key
    for i, (dz, y) in enumerate(ring_order()):
        src = ((z + sign * dz + Z) % Z) * Y + y
        for half in range(2):
            at = (2 * i + half) * SPAN
            visible = lead >= order[2 * src + half] * SPAN
            bias_ref[at : at + SPAN, :] = jnp.where(visible, 0.0, MASKED).astype(jnp.bfloat16)
    for copy in copies:
        copy.wait()


def prep(ids, order, queries):
    rows, width = queries.shape
    return pl.pallas_call(
        prep_kernel,
        out_shape=[
            jax.ShapeDtypeStruct((rows * (width // HEAD), 2 * HEAD), jnp.bfloat16),
            jax.ShapeDtypeStruct((Z * Y * rows, rows), jnp.bfloat16),
        ],
        in_specs=[SMEM, SMEM, HBM],
        out_specs=[VMEM, VMEM],
        scratch_shapes=[pltpu.SemaphoreType.DMA((width // HEAD,))],
        cost_estimate=pl.CostEstimate(flops=2 * 10**9, bytes_accessed=2 * 2**20, transcendentals=0),
        compiler_params=pltpu.CompilerParams(vmem_limit_bytes=16 * 2**20),
        name="prep",
    )(ids, order, queries)


def attend_kernel(start, n_kv, first, last, q_all, bias_ref, *refs):
    kv_refs, refs = refs[:n_kv], refs[n_kv:]
    if not first:
        acc_in, peak_in, refs = refs[0], refs[1], refs[2:]
    if last:
        w_ref, att_ref, part_ref = refs
    else:
        acc_out, peak_out = refs
    total, rows = q_all.shape[0], bias_ref.shape[1]
    k = jnp.concatenate([r[:, :, :HEAD].reshape(-1, HEAD) for r in kv_refs], axis=0)
    v = jnp.concatenate([r[:, :, HEAD:].reshape(-1, HEAD) for r in kv_refs], axis=0)
    k_ext = jnp.concatenate([k, bias_ref[start : start + k.shape[0], :]], axis=1)
    v_ext = jnp.concatenate([v, jnp.ones_like(v)], axis=1)
    for r in range(total // ROW_TILE):
        at = slice(r * ROW_TILE, (r + 1) * ROW_TILE)
        s = lax.dot_general(q_all[at, :], k_ext, (((1,), (1,)), ((), ())), preferred_element_type=jnp.float32)
        peak = jnp.max(s, axis=1, keepdims=True)
        if not first:
            old = peak_in[at, :1]
            peak = jnp.maximum(old, peak)
        p = jnp.exp2((s - peak) * EXP2_SCALE).astype(jnp.bfloat16)
        acc = jnp.dot(p, v_ext, preferred_element_type=jnp.float32)
        if not first:
            acc = acc + acc_in[at, :] * jnp.exp2((old - peak) * EXP2_SCALE)
        if last:
            att = (acc[:, :HEAD] / acc[:, HEAD:]).astype(jnp.bfloat16)
            for i in range(ROW_TILE // rows):
                h = r * ROW_TILE // rows + i
                att_ref[:, h * HEAD : (h + 1) * HEAD] = att[i * rows : (i + 1) * rows, :]
        else:
            acc_out[at, :] = acc
            peak_out[at, :] = jnp.broadcast_to(peak, (ROW_TILE, HEAD))
    if last:
        logits = jnp.dot(att_ref[...], w_ref[...], preferred_element_type=jnp.float32)
        part = rows // TP
        for t in range(TP):
            part_ref[t] = logits[t * part : (t + 1) * part, :].astype(jnp.bfloat16)


def attend(q_all, bias, kvs, start, state=None, readout=None):
    first, last = state is None, readout is not None
    total, rows = q_all.shape[0], bias.shape[1]
    keys = sum(kv.shape[0] * kv.shape[1] for kv in kvs)
    f32, b16 = jnp.float32, jnp.bfloat16
    args = [q_all, bias, *kvs]
    if not first:
        args += list(state)
    if last:
        vocab = readout.shape[1]
        args.append(readout)
        out = [
            jax.ShapeDtypeStruct((rows, total // rows * HEAD), b16),
            jax.ShapeDtypeStruct((TP, rows // TP, vocab), b16),
        ]
    else:
        out = [jax.ShapeDtypeStruct((total, 2 * HEAD), f32), jax.ShapeDtypeStruct((total, HEAD), f32)]
    return pl.pallas_call(
        functools.partial(attend_kernel, start, len(kvs), first, last),
        out_shape=out,
        in_specs=[VMEM] * len(args),
        out_specs=[VMEM] * len(out),
        cost_estimate=pl.CostEstimate(
            flops=COST * 4 * total * keys * 2 * HEAD, bytes_accessed=4 * 2**20, transcendentals=total * keys
        ),
        compiler_params=pltpu.CompilerParams(vmem_limit_bytes=24 * 2**20),
        name="attend_last" if last else "attend",
    )(*args)


def ratio_kernel(ids, part_ref, tok_ref, logp_ref, out_ref):
    f32 = jnp.float32
    _, part, vocab = part_ref.shape
    x = part_ref[0].astype(f32)
    for t in range(1, TP):
        x = x + part_ref[t].astype(f32)
    rows = tok_ref.shape[1]
    start = ids[1] * part
    mine = (
        lax.broadcasted_iota(jnp.int32, (part, rows), 0) + start
        == lax.broadcasted_iota(jnp.int32, (part, rows), 1)
    )
    token = jnp.sum(jnp.where(mine, tok_ref[...].astype(f32), 0.0), axis=1, keepdims=True).astype(jnp.int32)
    hit = lax.broadcasted_iota(jnp.int32, (part, vocab), 1) == token
    target = jnp.sum(jnp.where(hit, x, 0.0), axis=1, keepdims=True)
    peak = jnp.max(x, axis=1, keepdims=True)
    mass = jnp.sum(jnp.exp(x - peak), axis=1, keepdims=True)
    ratio = target - (peak + jnp.log(mass))
    out_ref[...] = jnp.sum(jnp.where(mine, ratio - logp_ref[...], 0.0), axis=0, keepdims=True)


def body(queries, keys, values, readout, token_ids, stored_logp, span_order):
    rows = queries.shape[0]
    ids = jnp.stack([lax.axis_index("ctx"), lax.axis_index("tp")]).astype(jnp.int32)
    q_all, bias = prep(ids, span_order, queries)

    kv = lax.all_to_all(pack(keys, values), "ctx", 0, 0, axis_index_groups=Y_GROUPS, tiled=True)
    kv, q_all, bias = lax.optimization_barrier((kv, q_all, bias))
    a, b = swap_z(kv, 0), swap_z(kv, 1)
    start = Y * rows
    state = attend(q_all, bias, [kv], 0)
    now = [a, b]
    a, b = swap_z(a, 1), swap_z(b, 0)
    for step in range(2, Z // 2 + 1):
        last = step == Z // 2
        state = attend(q_all, bias, now, start, state)
        start += 2 * Y * rows
        if last:
            break
        now = [a, b]
        if step == Z // 2 - 1:
            a, b = a[: Y // 2], b[Y // 2 :]
        a, b = swap_z(a, step % 2), swap_z(b, 1 - step % 2)
    attended, parts = attend(q_all, bias, [a, b], start, state, readout)

    parts = lax.all_to_all(parts, "tp", 0, 0, tiled=True)
    args = [parts, token_ids.reshape(1, rows), stored_logp.reshape(1, rows)]
    ratio = pl.pallas_call(
        ratio_kernel,
        out_shape=jax.ShapeDtypeStruct((1, rows), jnp.float32),
        in_specs=[SMEM] + [VMEM] * len(args),
        out_specs=VMEM,
        name="ratio",
    )(ids, *args)
    return attended, lax.psum(ratio.reshape(rows), "tp")


def solution(mesh):
    return jax.shard_map(
        body,
        mesh=mesh,
        in_specs=(
            P(("dp", "ctx"), "tp"),
            P(("dp", "ctx"), "tp"),
            P(("dp", "ctx"), "tp"),
            P("tp", None),
            P(("dp", "ctx")),
            P(("dp", "ctx")),
            P("dp"),
        ),
        out_specs=(P(("dp", "ctx"), "tp"), P(("dp", "ctx"))),
        check_vma=False,
    )
```

```python
import functools
import math

import jax
import jax.numpy as jnp
from jax import lax
from jax.experimental import pallas as pl
from jax.experimental.pallas import tpu as pltpu
from jax.sharding import PartitionSpec as P

HEAD = 128
Z = 8
Y = 4
TP = 4
SPAN = 64
ROW_TILE = 256
EXP2_SCALE = math.log2(math.e) / math.sqrt(HEAD)
MASKED = -1e30
COST = 4
Y_GROUPS = [[z * Y + y for y in range(Y)] for z in range(Z)]


def swap_z(x, odd):
    pairs = []
    for z in range(Z):
        partner = (z + (1 if z % 2 == odd else -1)) % Z
        pairs += [(z * Y + y, partner * Y + y) for y in range(Y)]
    return lax.ppermute(x, "ctx", pairs)


VMEM = pl.BlockSpec(memory_space=pltpu.VMEM)
SMEM = pl.BlockSpec(memory_space=pltpu.SMEM)
HBM = pl.BlockSpec(memory_space=pltpu.HBM)


def block(dz):
    return [(dz, y) for y in range(Y)]


def ring_order():
    order = block(0)
    for step in range(1, Z // 2):
        dz = step if step % 2 else -step
        order += block(dz) + block(-dz)
    return order + block(Z // 2)


def pack_kernel(k_ref, v_ref, out_ref, sems):
    copies = [
        pltpu.make_async_copy(k_ref, out_ref.at[0, :, pl.ds(0, HEAD)], sems.at[0]),
        pltpu.make_async_copy(v_ref, out_ref.at[0, :, pl.ds(HEAD, HEAD)], sems.at[1]),
    ]
    for copy in copies:
        copy.start()
    for copy in copies:
        copy.wait()
    for j in range(1, Y):
        out_ref[j] = out_ref[0]


def pack(keys, values):
    return pl.pallas_call(
        pack_kernel,
        out_shape=jax.ShapeDtypeStruct((Y, keys.shape[0], 2 * HEAD), keys.dtype),
        in_specs=[HBM] * 2,
        out_specs=VMEM,
        scratch_shapes=[pltpu.SemaphoreType.DMA((2,))],
        name="pack",
    )(keys, values)


def prep_kernel(ids, order, q_ref, q_all, bias_ref, sem):
    heads = q_ref.shape[1] // HEAD
    rows = q_ref.shape[0]
    copies = []
    for h in range(heads):
        copies.append(
            pltpu.make_async_copy(
                q_ref.at[:, pl.ds(h * HEAD, HEAD)], q_all.at[pl.ds(h * rows, rows), pl.ds(0, HEAD)], sem.at[h]
            )
        )
        copies[h].start()
    eye = (
        lax.broadcasted_iota(jnp.int32, (HEAD, HEAD), 0) == lax.broadcasted_iota(jnp.int32, (HEAD, HEAD), 1)
    ).astype(jnp.bfloat16)
    for h in range(heads):
        q_all[h * rows : (h + 1) * rows, HEAD:] = eye
    me = ids[0]
    z = me // Y
    sign = 1 - 2 * (z % 2)
    row = lax.broadcasted_iota(jnp.int32, (SPAN, 2 * SPAN), 1)
    key = lax.broadcasted_iota(jnp.int32, (SPAN, 2 * SPAN), 0)
    row_pos = jnp.where(row < SPAN, order[2 * me] * SPAN + row, order[2 * me + 1] * SPAN + row - SPAN)
    lead = row_pos - key
    for i, (dz, y) in enumerate(ring_order()):
        src = ((z + sign * dz + Z) % Z) * Y + y
        for half in range(2):
            at = (2 * i + half) * SPAN
            visible = lead >= order[2 * src + half] * SPAN
            bias_ref[at : at + SPAN, :] = jnp.where(visible, 0.0, MASKED).astype(jnp.bfloat16)
    for copy in copies:
        copy.wait()


def prep(ids, order, queries):
    rows, width = queries.shape
    return pl.pallas_call(
        prep_kernel,
        out_shape=[
            jax.ShapeDtypeStruct((rows * (width // HEAD), 2 * HEAD), jnp.bfloat16),
            jax.ShapeDtypeStruct((Z * Y * rows, rows), jnp.bfloat16),
        ],
        in_specs=[SMEM, SMEM, HBM],
        out_specs=[VMEM, VMEM],
        scratch_shapes=[pltpu.SemaphoreType.DMA((width // HEAD,))],
        cost_estimate=pl.CostEstimate(flops=2 * 10**9, bytes_accessed=2 * 2**20, transcendentals=0),
        compiler_params=pltpu.CompilerParams(vmem_limit_bytes=16 * 2**20),
        name="prep",
    )(ids, order, queries)


def attend_kernel(start, n_kv, first, last, q_all, bias_ref, *refs):
    kv_refs, refs = refs[:n_kv], refs[n_kv:]
    if not first:
        acc_in, peak_in, refs = refs[0], refs[1], refs[2:]
    if last:
        w_ref, att_ref, part_ref = refs
    else:
        acc_out, peak_out = refs
    total, rows = q_all.shape[0], bias_ref.shape[1]
    k = jnp.concatenate([r[:, :, :HEAD].reshape(-1, HEAD) for r in kv_refs], axis=0)
    v = jnp.concatenate([r[:, :, HEAD:].reshape(-1, HEAD) for r in kv_refs], axis=0)
    k_ext = jnp.concatenate([k, bias_ref[start : start + k.shape[0], :]], axis=1)
    v_ext = jnp.concatenate([v, jnp.ones_like(v)], axis=1)
    tiles = total // ROW_TILE

    def scores(r):
        at = slice(r * ROW_TILE, (r + 1) * ROW_TILE)
        return lax.dot_general(q_all[at, :], k_ext, (((1,), (1,)), ((), ())), preferred_element_type=jnp.float32)

    ahead = scores(0)
    for r in range(tiles):
        at = slice(r * ROW_TILE, (r + 1) * ROW_TILE)
        s = ahead
        if r + 1 < tiles:
            ahead = scores(r + 1)
        peak = jnp.max(s, axis=1, keepdims=True)
        if not first:
            old = peak_in[at, :1]
            peak = jnp.maximum(old, peak)
        p = jnp.exp2((s - peak) * EXP2_SCALE).astype(jnp.bfloat16)
        acc = jnp.dot(p, v_ext, preferred_element_type=jnp.float32)
        if not first:
            acc = acc + acc_in[at, :] * jnp.exp2((old - peak) * EXP2_SCALE)
        if last:
            att = (acc[:, :HEAD] / acc[:, HEAD:]).astype(jnp.bfloat16)
            for i in range(ROW_TILE // rows):
                h = r * ROW_TILE // rows + i
                att_ref[:, h * HEAD : (h + 1) * HEAD] = att[i * rows : (i + 1) * rows, :]
        else:
            acc_out[at, :] = acc
            peak_out[at, :] = jnp.broadcast_to(peak, (ROW_TILE, HEAD))
    if last:
        logits = jnp.dot(att_ref[...], w_ref[...], preferred_element_type=jnp.float32)
        part = rows // TP
        for t in range(TP):
            part_ref[t] = logits[t * part : (t + 1) * part, :].astype(jnp.bfloat16)


def attend(q_all, bias, kvs, start, state=None, readout=None):
    first, last = state is None, readout is not None
    total, rows = q_all.shape[0], bias.shape[1]
    keys = sum(kv.shape[0] * kv.shape[1] for kv in kvs)
    f32, b16 = jnp.float32, jnp.bfloat16
    args = [q_all, bias, *kvs]
    if not first:
        args += list(state)
    if last:
        vocab = readout.shape[1]
        args.append(readout)
        out = [
            jax.ShapeDtypeStruct((rows, total // rows * HEAD), b16),
            jax.ShapeDtypeStruct((TP, rows // TP, vocab), b16),
        ]
    else:
        out = [jax.ShapeDtypeStruct((total, 2 * HEAD), f32), jax.ShapeDtypeStruct((total, HEAD), f32)]
    return pl.pallas_call(
        functools.partial(attend_kernel, start, len(kvs), first, last),
        out_shape=out,
        in_specs=[VMEM] * len(args),
        out_specs=[VMEM] * len(out),
        cost_estimate=pl.CostEstimate(
            flops=COST * 4 * total * keys * 2 * HEAD, bytes_accessed=4 * 2**20, transcendentals=total * keys
        ),
        compiler_params=pltpu.CompilerParams(vmem_limit_bytes=24 * 2**20),
        name="attend_last" if last else "attend",
    )(*args)


def ratio_kernel(ids, part_ref, tok_ref, logp_ref, out_ref):
    f32 = jnp.float32
    _, part, vocab = part_ref.shape
    x = part_ref[0].astype(f32)
    for t in range(1, TP):
        x = x + part_ref[t].astype(f32)
    rows = tok_ref.shape[1]
    start = ids[1] * part
    mine = (
        lax.broadcasted_iota(jnp.int32, (part, rows), 0) + start
        == lax.broadcasted_iota(jnp.int32, (part, rows), 1)
    )
    token = jnp.sum(jnp.where(mine, tok_ref[...].astype(f32), 0.0), axis=1, keepdims=True).astype(jnp.int32)
    hit = lax.broadcasted_iota(jnp.int32, (part, vocab), 1) == token
    target = jnp.sum(jnp.where(hit, x, 0.0), axis=1, keepdims=True)
    peak = jnp.max(x, axis=1, keepdims=True)
    mass = jnp.sum(jnp.exp(x - peak), axis=1, keepdims=True)
    ratio = target - (peak + jnp.log(mass))
    mine_row = jnp.sum(jnp.where(mine, ratio - logp_ref[...], 0.0), axis=0, keepdims=True)
    out_ref[...] = jnp.broadcast_to(mine_row[None], out_ref.shape)


def body(queries, keys, values, readout, token_ids, stored_logp, span_order):
    rows = queries.shape[0]
    ids = jnp.stack([lax.axis_index(axis) for axis in ("ctx", "tp")]).astype(jnp.int32)
    q_all, bias = prep(ids, span_order, queries)

    kv = lax.all_to_all(pack(keys, values), "ctx", 0, 0, axis_index_groups=Y_GROUPS, tiled=True)
    kv, q_all, bias = lax.optimization_barrier((kv, q_all, bias))
    a, b = swap_z(kv, 0), swap_z(kv, 1)
    per = Y * rows
    state = attend(q_all, bias, [kv], 0)
    a2, b2 = swap_z(a, 1), swap_z(b, 0)
    _, state = lax.optimization_barrier((a2, state))
    state = attend(q_all, bias, [a, b], per, state)
    a3 = swap_z(a2, 0)
    held, state = lax.optimization_barrier((b2, state))
    b3 = swap_z(held, 1)
    _, state = lax.optimization_barrier((a3, state))
    state = attend(q_all, bias, [a2, b2], 3 * per, state)
    a4 = swap_z(a3, 1)
    state = attend(q_all, bias, [a3, b3], 5 * per, state)
    attended, parts = attend(q_all, bias, [a4], 7 * per, state, readout)

    parts = lax.all_to_all(parts, "tp", 0, 0, tiled=True)
    args = [parts, token_ids.reshape(1, rows), stored_logp.reshape(1, rows)]
    ratio = pl.pallas_call(
        ratio_kernel,
        out_shape=jax.ShapeDtypeStruct((TP, 1, rows), jnp.float32),
        in_specs=[SMEM] + [VMEM] * len(args),
        out_specs=VMEM,
        name="ratio",
    )(ids, *args)
    ratio = lax.all_to_all(ratio, "tp", 0, 0, tiled=True)
    return attended, jnp.sum(ratio, axis=(0, 1))


def solution(mesh):
    return jax.shard_map(
        body,
        mesh=mesh,
        in_specs=(
            P(("dp", "ctx"), "tp"),
            P(("dp", "ctx"), "tp"),
            P(("dp", "ctx"), "tp"),
            P("tp", None),
            P(("dp", "ctx")),
            P(("dp", "ctx")),
            P("dp"),
        ),
        out_specs=(P(("dp", "ctx"), "tp"), P(("dp", "ctx"))),
        check_vma=False,
    )
```

```python
import functools
import math

import jax
import jax.numpy as jnp
from jax import lax
from jax.experimental import pallas as pl
from jax.experimental.pallas import tpu as pltpu
from jax.sharding import PartitionSpec as P

HEAD = 128
Z = 8
Y = 4
TP = 4
SPAN = 64
ROW_TILE = 256
EXP2_SCALE = math.log2(math.e) / math.sqrt(HEAD)
MASKED = -1e30
COST = 4
Y_GROUPS = [[z * Y + y for y in range(Y)] for z in range(Z)]


def swap_z(x, odd):
    pairs = []
    for z in range(Z):
        partner = (z + (1 if z % 2 != odd else -1)) % Z
        pairs += [(z * Y + y, partner * Y + y) for y in range(Y)]
    return lax.ppermute(x, "ctx", pairs)


VMEM = pl.BlockSpec(memory_space=pltpu.VMEM)
SMEM = pl.BlockSpec(memory_space=pltpu.SMEM)
HBM = pl.BlockSpec(memory_space=pltpu.HBM)


def block(dz):
    return [(dz, y) for y in range(Y)]


def ring_order():
    order = block(0)
    for step in range(1, Z // 2):
        dz = step if step % 2 else -step
        order += block(dz) + block(-dz)
    return order + block(Z // 2)


def pack_kernel(k_ref, v_ref, out_ref, sems):
    copies = [
        pltpu.make_async_copy(k_ref, out_ref.at[0, :, pl.ds(0, HEAD)], sems.at[0]),
        pltpu.make_async_copy(v_ref, out_ref.at[0, :, pl.ds(HEAD, HEAD)], sems.at[1]),
    ]
    for copy in copies:
        copy.start()
    for copy in copies:
        copy.wait()
    for j in range(1, Y):
        out_ref[j] = out_ref[0]


def pack(keys, values):
    return pl.pallas_call(
        pack_kernel,
        out_shape=jax.ShapeDtypeStruct((Y, keys.shape[0], 2 * HEAD), keys.dtype),
        in_specs=[HBM] * 2,
        out_specs=VMEM,
        scratch_shapes=[pltpu.SemaphoreType.DMA((2,))],
        name="pack",
    )(keys, values)


def prep_kernel(ids, order, q_ref, q_all, bias_ref, sem):
    heads = q_ref.shape[1] // HEAD
    rows = q_ref.shape[0]
    copies = []
    for h in range(heads):
        copies.append(
            pltpu.make_async_copy(
                q_ref.at[:, pl.ds(h * HEAD, HEAD)], q_all.at[pl.ds(h * rows, rows), pl.ds(0, HEAD)], sem.at[h]
            )
        )
        copies[h].start()
    eye = (
        lax.broadcasted_iota(jnp.int32, (HEAD, HEAD), 0) == lax.broadcasted_iota(jnp.int32, (HEAD, HEAD), 1)
    ).astype(jnp.bfloat16)
    for h in range(heads):
        q_all[h * rows : (h + 1) * rows, HEAD:] = eye
    me = ids[0]
    z = me // Y
    sign = 2 * (z % 2) - 1
    row = lax.broadcasted_iota(jnp.int32, (SPAN, 2 * SPAN), 1)
    key = lax.broadcasted_iota(jnp.int32, (SPAN, 2 * SPAN), 0)
    row_pos = jnp.where(row < SPAN, order[2 * me] * SPAN + row, order[2 * me + 1] * SPAN + row - SPAN)
    lead = row_pos - key
    for i, (dz, y) in enumerate(ring_order()):
        src = ((z + sign * dz + Z) % Z) * Y + y
        for half in range(2):
            at = (2 * i + half) * SPAN
            visible = lead >= order[2 * src + half] * SPAN
            bias_ref[at : at + SPAN, :] = jnp.where(visible, 0.0, MASKED).astype(jnp.bfloat16)
    for copy in copies:
        copy.wait()


def prep(ids, order, queries):
    rows, width = queries.shape
    return pl.pallas_call(
        prep_kernel,
        out_shape=[
            jax.ShapeDtypeStruct((rows * (width // HEAD), 2 * HEAD), jnp.bfloat16),
            jax.ShapeDtypeStruct((Z * Y * rows, rows), jnp.bfloat16),
        ],
        in_specs=[SMEM, SMEM, HBM],
        out_specs=[VMEM, VMEM],
        scratch_shapes=[pltpu.SemaphoreType.DMA((width // HEAD,))],
        cost_estimate=pl.CostEstimate(flops=2 * 10**9, bytes_accessed=2 * 2**20, transcendentals=0),
        compiler_params=pltpu.CompilerParams(vmem_limit_bytes=16 * 2**20),
        name="prep",
    )(ids, order, queries)


def attend_kernel(start, n_kv, first, last, q_all, bias_ref, *refs):
    kv_refs, refs = refs[:n_kv], refs[n_kv:]
    if not first:
        acc_in, peak_in, refs = refs[0], refs[1], refs[2:]
    if last:
        w_ref, att_ref, part_ref = refs
    else:
        acc_out, peak_out = refs
    total, rows = q_all.shape[0], bias_ref.shape[1]
    k = jnp.concatenate([r[:, :, :HEAD].reshape(-1, HEAD) for r in kv_refs], axis=0)
    v = jnp.concatenate([r[:, :, HEAD:].reshape(-1, HEAD) for r in kv_refs], axis=0)
    k_ext = jnp.concatenate([k, bias_ref[start : start + k.shape[0], :]], axis=1)
    v_ext = jnp.concatenate([v, jnp.ones_like(v)], axis=1)
    tiles = total // ROW_TILE

    def scores(r):
        at = slice(r * ROW_TILE, (r + 1) * ROW_TILE)
        return lax.dot_general(q_all[at, :], k_ext, (((1,), (1,)), ((), ())), preferred_element_type=jnp.float32)

    ahead = scores(0)
    for r in range(tiles):
        at = slice(r * ROW_TILE, (r + 1) * ROW_TILE)
        s = ahead
        if r + 1 < tiles:
            ahead = scores(r + 1)
        peak = jnp.max(s, axis=1, keepdims=True)
        if not first:
            old = peak_in[at, :1]
            peak = jnp.maximum(old, peak)
        p = jnp.exp2((s - peak) * EXP2_SCALE).astype(jnp.bfloat16)
        acc = jnp.dot(p, v_ext, preferred_element_type=jnp.float32)
        if not first:
            acc = acc + acc_in[at, :] * jnp.exp2((old - peak) * EXP2_SCALE)
        if last:
            att = (acc[:, :HEAD] / acc[:, HEAD:]).astype(jnp.bfloat16)
            for i in range(ROW_TILE // rows):
                h = r * ROW_TILE // rows + i
                att_ref[:, h * HEAD : (h + 1) * HEAD] = att[i * rows : (i + 1) * rows, :]
        else:
            acc_out[at, :] = acc
            peak_out[at, :] = jnp.broadcast_to(peak, (ROW_TILE, HEAD))
    if last:
        logits = jnp.dot(att_ref[...], w_ref[...], preferred_element_type=jnp.float32)
        part = rows // TP
        for t in range(TP):
            part_ref[t] = logits[t * part : (t + 1) * part, :].astype(jnp.bfloat16)


def attend(q_all, bias, kvs, start, state=None, readout=None):
    first, last = state is None, readout is not None
    total, rows = q_all.shape[0], bias.shape[1]
    keys = sum(kv.shape[0] * kv.shape[1] for kv in kvs)
    f32, b16 = jnp.float32, jnp.bfloat16
    args = [q_all, bias, *kvs]
    if not first:
        args += list(state)
    if last:
        vocab = readout.shape[1]
        args.append(readout)
        out = [
            jax.ShapeDtypeStruct((rows, total // rows * HEAD), b16),
            jax.ShapeDtypeStruct((TP, rows // TP, vocab), b16),
        ]
    else:
        out = [jax.ShapeDtypeStruct((total, 2 * HEAD), f32), jax.ShapeDtypeStruct((total, HEAD), f32)]
    return pl.pallas_call(
        functools.partial(attend_kernel, start, len(kvs), first, last),
        out_shape=out,
        in_specs=[VMEM] * len(args),
        out_specs=[VMEM] * len(out),
        cost_estimate=pl.CostEstimate(
            flops=COST * 4 * total * keys * 2 * HEAD, bytes_accessed=4 * 2**20, transcendentals=total * keys
        ),
        compiler_params=pltpu.CompilerParams(vmem_limit_bytes=24 * 2**20),
        name="attend_last" if last else "attend",
    )(*args)


def ratio_kernel(ids, part_ref, tok_ref, logp_ref, out_ref):
    f32 = jnp.float32
    _, part, vocab = part_ref.shape
    x = part_ref[0].astype(f32)
    for t in range(1, TP):
        x = x + part_ref[t].astype(f32)
    rows = tok_ref.shape[1]
    start = ids[1] * part
    mine = (
        lax.broadcasted_iota(jnp.int32, (part, rows), 0) + start
        == lax.broadcasted_iota(jnp.int32, (part, rows), 1)
    )
    token = jnp.sum(jnp.where(mine, tok_ref[...].astype(f32), 0.0), axis=1, keepdims=True).astype(jnp.int32)
    hit = lax.broadcasted_iota(jnp.int32, (part, vocab), 1) == token
    target = jnp.sum(jnp.where(hit, x, 0.0), axis=1, keepdims=True)
    peak = jnp.max(x, axis=1, keepdims=True)
    mass = jnp.sum(jnp.exp(x - peak), axis=1, keepdims=True)
    ratio = target - (peak + jnp.log(mass))
    mine_row = jnp.sum(jnp.where(mine, ratio - logp_ref[...], 0.0), axis=0, keepdims=True)
    out_ref[...] = jnp.broadcast_to(mine_row[None], out_ref.shape)


def body(queries, keys, values, readout, token_ids, stored_logp, span_order):
    rows = queries.shape[0]
    ids = jnp.stack([lax.axis_index(axis) for axis in ("ctx", "tp")]).astype(jnp.int32)
    q_all, bias = prep(ids, span_order, queries)

    kv = lax.all_to_all(pack(keys, values), "ctx", 0, 0, axis_index_groups=Y_GROUPS, tiled=True)
    kv, q_all, bias = lax.optimization_barrier((kv, q_all, bias))
    a, b = swap_z(kv, 0), swap_z(kv, 1)
    per = Y * rows
    state = attend(q_all, bias, [kv], 0)
    a2, b2 = swap_z(a, 1), swap_z(b, 0)
    _, state = lax.optimization_barrier((a2, state))
    state = attend(q_all, bias, [a, b], per, state)
    a3 = swap_z(a2, 0)
    held, state = lax.optimization_barrier((b2, state))
    b3 = swap_z(held, 1)
    _, state = lax.optimization_barrier((a3, state))
    state = attend(q_all, bias, [a2, b2], 3 * per, state)
    a4 = swap_z(a3, 1)
    state = attend(q_all, bias, [a3, b3], 5 * per, state)
    attended, parts = attend(q_all, bias, [a4], 7 * per, state, readout)

    parts = lax.all_to_all(parts, "tp", 0, 0, tiled=True)
    args = [parts, token_ids.reshape(1, rows), stored_logp.reshape(1, rows)]
    ratio = pl.pallas_call(
        ratio_kernel,
        out_shape=jax.ShapeDtypeStruct((TP, 1, rows), jnp.float32),
        in_specs=[SMEM] + [VMEM] * len(args),
        out_specs=VMEM,
        name="ratio",
    )(ids, *args)
    ratio = lax.all_to_all(ratio, "tp", 0, 0, tiled=True)
    return attended, jnp.sum(ratio, axis=(0, 1))


def solution(mesh):
    return jax.shard_map(
        body,
        mesh=mesh,
        in_specs=(
            P(("dp", "ctx"), "tp"),
            P(("dp", "ctx"), "tp"),
            P(("dp", "ctx"), "tp"),
            P("tp", None),
            P(("dp", "ctx")),
            P(("dp", "ctx")),
            P("dp"),
        ),
        out_specs=(P(("dp", "ctx"), "tp"), P(("dp", "ctx"))),
        check_vma=False,
    )
```

```python
import functools
import math

import jax
import jax.numpy as jnp
from jax import lax
from jax.experimental import pallas as pl
from jax.experimental.pallas import tpu as pltpu
from jax.sharding import PartitionSpec as P

HEAD = 128
Z = 8
Y = 4
TP = 4
SPAN = 64
ROW_TILE = 512
EXP2_SCALE = math.log2(math.e) / math.sqrt(HEAD)
MASKED = -1e30
COST = 4
Y_GROUPS = [[z * Y + y for y in range(Y)] for z in range(Z)]


def swap_z(x, odd):
    pairs = []
    for z in range(Z):
        partner = (z + (1 if z % 2 != odd else -1)) % Z
        pairs += [(z * Y + y, partner * Y + y) for y in range(Y)]
    return lax.ppermute(x, "ctx", pairs)


VMEM = pl.BlockSpec(memory_space=pltpu.VMEM)
SMEM = pl.BlockSpec(memory_space=pltpu.SMEM)
HBM = pl.BlockSpec(memory_space=pltpu.HBM)


def block(dz):
    return [(dz, y) for y in range(Y)]


def ring_order():
    order = block(0)
    for step in range(1, Z // 2):
        dz = step if step % 2 else -step
        order += block(dz) + block(-dz)
    return order + block(Z // 2)


def pack_kernel(k_ref, v_ref, out_ref, sems):
    copies = [
        pltpu.make_async_copy(k_ref, out_ref.at[0, :, pl.ds(0, HEAD)], sems.at[0]),
        pltpu.make_async_copy(v_ref, out_ref.at[0, :, pl.ds(HEAD, HEAD)], sems.at[1]),
    ]
    for copy in copies:
        copy.start()
    for copy in copies:
        copy.wait()
    for j in range(1, Y):
        out_ref[j] = out_ref[0]


def pack(keys, values):
    return pl.pallas_call(
        pack_kernel,
        out_shape=jax.ShapeDtypeStruct((Y, keys.shape[0], 2 * HEAD), keys.dtype),
        in_specs=[HBM] * 2,
        out_specs=VMEM,
        scratch_shapes=[pltpu.SemaphoreType.DMA((2,))],
        name="pack",
    )(keys, values)


def prep_kernel(ids, order, q_ref, q_all, bias_ref, sem):
    heads = q_ref.shape[1] // HEAD
    rows = q_ref.shape[0]
    copies = []
    for h in range(heads):
        copies.append(
            pltpu.make_async_copy(
                q_ref.at[:, pl.ds(h * HEAD, HEAD)], q_all.at[pl.ds(h * rows, rows), pl.ds(0, HEAD)], sem.at[h]
            )
        )
        copies[h].start()
    eye = (
        lax.broadcasted_iota(jnp.int32, (HEAD, HEAD), 0) == lax.broadcasted_iota(jnp.int32, (HEAD, HEAD), 1)
    ).astype(jnp.bfloat16)
    for h in range(heads):
        q_all[h * rows : (h + 1) * rows, HEAD:] = eye
    me = ids[0]
    z = me // Y
    sign = 2 * (z % 2) - 1
    row = lax.broadcasted_iota(jnp.int32, (SPAN, 2 * SPAN), 1)
    key = lax.broadcasted_iota(jnp.int32, (SPAN, 2 * SPAN), 0)
    row_pos = jnp.where(row < SPAN, order[2 * me] * SPAN + row, order[2 * me + 1] * SPAN + row - SPAN)
    lead = row_pos - key
    for i, (dz, y) in enumerate(ring_order()):
        src = ((z + sign * dz + Z) % Z) * Y + y
        for half in range(2):
            at = (2 * i + half) * SPAN
            visible = lead >= order[2 * src + half] * SPAN
            bias_ref[at : at + SPAN, :] = jnp.where(visible, 0.0, MASKED).astype(jnp.bfloat16)
    for copy in copies:
        copy.wait()


def prep(ids, order, queries):
    rows, width = queries.shape
    return pl.pallas_call(
        prep_kernel,
        out_shape=[
            jax.ShapeDtypeStruct((rows * (width // HEAD), 2 * HEAD), jnp.bfloat16),
            jax.ShapeDtypeStruct((Z * Y * rows, rows), jnp.bfloat16),
        ],
        in_specs=[SMEM, SMEM, HBM],
        out_specs=[VMEM, VMEM],
        scratch_shapes=[pltpu.SemaphoreType.DMA((width // HEAD,))],
        cost_estimate=pl.CostEstimate(flops=2 * 10**9, bytes_accessed=2 * 2**20, transcendentals=0),
        compiler_params=pltpu.CompilerParams(vmem_limit_bytes=16 * 2**20),
        name="prep",
    )(ids, order, queries)


def attend_kernel(start, n_kv, first, last, q_all, bias_ref, *refs):
    kv_refs, refs = refs[:n_kv], refs[n_kv:]
    if not first:
        acc_in, peak_in, refs = refs[0], refs[1], refs[2:]
    if last:
        w_ref, att_ref, part_ref = refs
    else:
        acc_out, peak_out = refs
    total, rows = q_all.shape[0], bias_ref.shape[1]
    k = jnp.concatenate([r[:, :, :HEAD].reshape(-1, HEAD) for r in kv_refs], axis=0)
    v = jnp.concatenate([r[:, :, HEAD:].reshape(-1, HEAD) for r in kv_refs], axis=0)
    k_ext = jnp.concatenate([k, bias_ref[start : start + k.shape[0], :]], axis=1)
    v_ext = jnp.concatenate([v, jnp.ones_like(v)], axis=1)
    tiles = total // ROW_TILE

    def scores(r):
        at = slice(r * ROW_TILE, (r + 1) * ROW_TILE)
        return lax.dot_general(q_all[at, :], k_ext, (((1,), (1,)), ((), ())), preferred_element_type=jnp.float32)

    ahead = scores(0)
    for r in range(tiles):
        at = slice(r * ROW_TILE, (r + 1) * ROW_TILE)
        s = ahead
        if r + 1 < tiles:
            ahead = scores(r + 1)
        peak = jnp.max(s, axis=1, keepdims=True)
        if not first:
            old = peak_in[at, :1]
            peak = jnp.maximum(old, peak)
        p = jnp.exp2((s - peak) * EXP2_SCALE).astype(jnp.bfloat16)
        acc = jnp.dot(p, v_ext, preferred_element_type=jnp.float32)
        if not first:
            acc = acc + acc_in[at, :] * jnp.exp2((old - peak) * EXP2_SCALE)
        if last:
            att = (acc[:, :HEAD] / acc[:, HEAD:]).astype(jnp.bfloat16)
            for i in range(ROW_TILE // rows):
                h = r * ROW_TILE // rows + i
                att_ref[:, h * HEAD : (h + 1) * HEAD] = att[i * rows : (i + 1) * rows, :]
        else:
            acc_out[at, :] = acc
            peak_out[at, :] = jnp.broadcast_to(peak, (ROW_TILE, HEAD))
    if last:
        logits = jnp.dot(att_ref[...], w_ref[...], preferred_element_type=jnp.float32)
        part = rows // TP
        for t in range(TP):
            part_ref[t] = logits[t * part : (t + 1) * part, :].astype(jnp.bfloat16)


def attend(q_all, bias, kvs, start, state=None, readout=None):
    first, last = state is None, readout is not None
    total, rows = q_all.shape[0], bias.shape[1]
    keys = sum(kv.shape[0] * kv.shape[1] for kv in kvs)
    f32, b16 = jnp.float32, jnp.bfloat16
    args = [q_all, bias, *kvs]
    if not first:
        args += list(state)
    if last:
        vocab = readout.shape[1]
        args.append(readout)
        out = [
            jax.ShapeDtypeStruct((rows, total // rows * HEAD), b16),
            jax.ShapeDtypeStruct((TP, rows // TP, vocab), b16),
        ]
    else:
        out = [jax.ShapeDtypeStruct((total, 2 * HEAD), f32), jax.ShapeDtypeStruct((total, HEAD), f32)]
    return pl.pallas_call(
        functools.partial(attend_kernel, start, len(kvs), first, last),
        out_shape=out,
        in_specs=[VMEM] * len(args),
        out_specs=[VMEM] * len(out),
        cost_estimate=pl.CostEstimate(
            flops=COST * 4 * total * keys * 2 * HEAD, bytes_accessed=4 * 2**20, transcendentals=total * keys
        ),
        compiler_params=pltpu.CompilerParams(vmem_limit_bytes=24 * 2**20),
        name="attend_last" if last else "attend",
    )(*args)


def ratio_kernel(ids, part_ref, tok_ref, logp_ref, out_ref):
    f32 = jnp.float32
    _, part, vocab = part_ref.shape
    x = part_ref[0].astype(f32)
    for t in range(1, TP):
        x = x + part_ref[t].astype(f32)
    rows = tok_ref.shape[1]
    start = ids[1] * part
    mine = (
        lax.broadcasted_iota(jnp.int32, (part, rows), 0) + start
        == lax.broadcasted_iota(jnp.int32, (part, rows), 1)
    )
    token = jnp.sum(jnp.where(mine, tok_ref[...].astype(f32), 0.0), axis=1, keepdims=True).astype(jnp.int32)
    hit = lax.broadcasted_iota(jnp.int32, (part, vocab), 1) == token
    target = jnp.sum(jnp.where(hit, x, 0.0), axis=1, keepdims=True)
    peak = jnp.max(x, axis=1, keepdims=True)
    mass = jnp.sum(jnp.exp(x - peak), axis=1, keepdims=True)
    ratio = target - (peak + jnp.log(mass))
    mine_row = jnp.sum(jnp.where(mine, ratio - logp_ref[...], 0.0), axis=0, keepdims=True)
    out_ref[...] = jnp.broadcast_to(mine_row[None], out_ref.shape)


def body(queries, keys, values, readout, token_ids, stored_logp, span_order):
    rows = queries.shape[0]
    ids = jnp.stack([lax.axis_index(axis) for axis in ("ctx", "tp")]).astype(jnp.int32)
    q_all, bias = prep(ids, span_order, queries)

    kv = lax.all_to_all(pack(keys, values), "ctx", 0, 0, axis_index_groups=Y_GROUPS, tiled=True)
    kv, q_all, bias = lax.optimization_barrier((kv, q_all, bias))
    a, b = swap_z(kv, 0), swap_z(kv, 1)
    per = Y * rows
    state = attend(q_all, bias, [kv], 0)
    a2, b2 = swap_z(a, 1), swap_z(b, 0)
    _, state = lax.optimization_barrier((a2, state))
    state = attend(q_all, bias, [a, b], per, state)
    a3 = swap_z(a2, 0)
    held, state = lax.optimization_barrier((b2, state))
    b3 = swap_z(held, 1)
    _, state = lax.optimization_barrier((a3, state))
    state = attend(q_all, bias, [a2, b2], 3 * per, state)
    a4 = swap_z(a3, 1)
    state = attend(q_all, bias, [a3, b3], 5 * per, state)
    attended, parts = attend(q_all, bias, [a4], 7 * per, state, readout)

    parts = lax.all_to_all(parts, "tp", 0, 0, tiled=True)
    args = [parts, token_ids.reshape(1, rows), stored_logp.reshape(1, rows)]
    ratio = pl.pallas_call(
        ratio_kernel,
        out_shape=jax.ShapeDtypeStruct((TP, 1, rows), jnp.float32),
        in_specs=[SMEM] + [VMEM] * len(args),
        out_specs=VMEM,
        name="ratio",
    )(ids, *args)
    ratio = lax.all_to_all(ratio, "tp", 0, 0, tiled=True)
    return attended, jnp.sum(ratio, axis=(0, 1))


def solution(mesh):
    return jax.shard_map(
        body,
        mesh=mesh,
        in_specs=(
            P(("dp", "ctx"), "tp"),
            P(("dp", "ctx"), "tp"),
            P(("dp", "ctx"), "tp"),
            P("tp", None),
            P(("dp", "ctx")),
            P(("dp", "ctx")),
            P("dp"),
        ),
        out_specs=(P(("dp", "ctx"), "tp"), P(("dp", "ctx"))),
        check_vma=False,
    )
```
